32 devices in a mesh: row: 8 (over y, x, core), tensor: 4 (over z).
Axes of the slice: x: 2, y: 2, z: 4, core: 2. Of those that a mesh axis runs over, the one named last changes fastest.
Arguments:
- hidden_rows: bfloat16 [2048, 8192], P('row'), may hold values from -6 to 6
- w_query: bfloat16 [8192, 8192], P('row', 'tensor'), may hold values from -0.0625 to 0.0625
- w_out: bfloat16 [8192, 8192], P('tensor', 'row'), may hold values from -0.0625 to 0.0625
- pack_key_cache: bfloat16 [65536, 1024], P('row', 'tensor'), may hold values from -250 to 250
- pack_value_cache: bfloat16 [65536, 1024], P('row', 'tensor'), may hold values from -6 to 6
- query_pos: int32 [2048], P('row'), may hold values from 0 to 65535, as said below
- doc_blocks: int32 [8, 4], P('row'), may hold values from 1 to 32, 64 in all within a row
Outputs:
- mixed: bfloat16 [2048, 8192], P('row', 'tensor')
The draws below stay inside these ranges and needn't reach their ends.
Inputs may be any that keep to these rules, and one draw needn't show every extreme that they name: `query_pos`: each index of row holds 256 consecutive query rows; at most 64 of them lie in any one block of 8192 key positions, and exactly 64 in some blocks. Positions may repeat. `doc_blocks`: each row sums to 64.
All inputs are finite; a program needn't handle non-finite values.
Results may differ from the reference program's by a relative error of at most 0.014.
The reference program's roundings to bfloat16 on the way count: a program that leaves them out, or rounds other values in their place, can miss the bound.
Values may be sent and summed in bfloat16 or wider, within the bound.
A program may use at most 192 MiB of HBM per device.

```python
import math
import jax
import jax.numpy as jnp
import numpy as np
from jax import lax

D = 8192
QUERY_HEADS = 64
KEY_VALUE_HEADS = 8
HEAD_SIZE = 128
QRY_DEV = 256
KEY_DEV = 8192
DOCS = 4
QROWS = 2048
KEY_POSITIONS = 65536
N_ROW = 8
N_TENSOR = 4


def draw_query_pos(key, part):
    capacity = 2 * QRY_DEV // N_ROW
    rank_key, noise_key, perm_key, offset_key = jax.random.split(key, 4)
    global_rank = jax.random.permutation(rank_key, N_ROW).astype(jnp.int32)
    noise = jax.random.randint(noise_key, (N_ROW, N_ROW), 0, 2 * N_ROW).astype(jnp.int32)
    server_ids = jnp.arange(N_ROW, dtype=jnp.int32)
    ranking = (global_rank[None, :] + noise) * N_ROW + server_ids[None, :]
    order = jnp.argsort(ranking, axis=1, stable=True).astype(jnp.int32)
    levels = jnp.where(server_ids < N_ROW // 4, capacity, jnp.where(server_ids < N_ROW // 2, capacity // 2, capacity // 4)).astype(jnp.int32)
    counts = jnp.zeros((N_ROW, N_ROW), jnp.int32).at[server_ids[:, None], order].set(jnp.broadcast_to(levels[None, :], (N_ROW, N_ROW)))

    def one_source(count_row, source_key):
        listed = jnp.repeat(server_ids, count_row, total_repeat_length=QRY_DEV)
        return jax.random.permutation(source_key, listed)
    source_keys = jax.random.split(perm_key, N_ROW)
    target_server = jax.vmap(one_source)(counts, source_keys)
    offsets = jax.random.randint(offset_key, (N_ROW, QRY_DEV), 0, KEY_DEV).astype(jnp.int32)
    return (target_server * KEY_DEV + offsets).reshape(QROWS).astype(jnp.int32)


def draw_pack_key_cache(key, part):
    base_key = jax.random.fold_in(jax.random.fold_in(key, 7), 0)
    array_shape = (KEY_POSITIONS, KEY_VALUE_HEADS * HEAD_SIZE)
    base = jax.random.normal(base_key, array_shape, jnp.float32)
    return jnp.clip(base, -6.0, 6.0).astype(jnp.bfloat16)


def block_levels(own_key, shape, cuts, least, largest):
    level, own = 1.0, jax.random.fold_in(own_key, 6)
    for axis_at, parts in cuts:
        heights = jnp.exp(jax.random.uniform(jax.random.fold_in(own, axis_at), (parts,), jnp.float32, least / len(cuts), largest / len(cuts)))
        level = level * jnp.repeat(heights, shape[axis_at] // parts).reshape([-1 if axis == axis_at else 1 for axis in range(len(shape))])
    return level


def length_profile(amount, total, reach, slope):
    weights = [(1 << 20) // math.isqrt(standing ** slope) + 1 for standing in range(2, amount + 1)]
    surplus, given = total - reach - (amount - 1), [1] * (amount - 1)
    while surplus > 0:
        free = [i for i in range(amount - 1) if given[i] < reach]
        whole, remaining = sum([weights[i] for i in free]), surplus
        for i in free:
            extra = min(reach - given[i], max(1, remaining * weights[i] // whole), surplus)
            given[i] = given[i] + extra
            surplus = surplus - extra
    return np.array([reach] + given)


def uneven(key, amount, total, bound, skew):
    if amount == 2:
        one = jax.random.randint(key, (), max(1, total - bound), min(bound, total - 1) + 1)
        return jnp.stack([one, total - one])
    sizes = jnp.asarray(length_profile(amount, total, bound, skew), jnp.int32)
    couples = (amount - 1) // 2
    source_of, receiver = sizes[1:1 + 2 * couples:2], sizes[2:2 + 2 * couples:2]
    room = jnp.minimum(source_of - 1, bound - receiver)
    shifted = jax.random.randint(jax.random.fold_in(key, 1), (couples,), 0, 1 << 20) % (room + 1)
    sizes = sizes.at[1:1 + 2 * couples:2].set(source_of - shifted).at[2:2 + 2 * couples:2].set(receiver + shifted)
    return sizes[jax.random.permutation(jax.random.fold_in(key, 2), amount)]


def bell_draw(stream_key, extent, spread, limit, cuts=(), kind=jnp.bfloat16):
    drawn = spread * jax.random.normal(stream_key, extent, jnp.float32)
    if cuts:
        drawn = drawn * block_levels(stream_key, extent, cuts, -0.22, 0.18)
    return jnp.clip(drawn, -limit, limit).astype(kind)


def setup_inputs(seed: int = 0) -> dict:
    key_of = jax.random.split(jax.random.key(seed), 8)
    return {
        "hidden_rows": bell_draw(key_of[0], (QROWS, D), 1.0, 6.0, ((0, 8),)),
        "w_query": bell_draw(key_of[1], (D, QUERY_HEADS * HEAD_SIZE), D ** -0.5, 0.0625, ((0, 8), (1, 4))),
        "w_out": bell_draw(key_of[2], (QUERY_HEADS * HEAD_SIZE, D), (QUERY_HEADS * HEAD_SIZE) ** -0.5, 0.0625, ((0, 4), (1, 8))),
        "pack_key_cache": draw_pack_key_cache(jax.random.fold_in(key_of[7], 71), 0),
        "pack_value_cache": bell_draw(key_of[4], (KEY_POSITIONS, KEY_VALUE_HEADS * HEAD_SIZE), 1.0, 6.0, ((0, 8), (1, 4))),
        "query_pos": draw_query_pos(jax.random.fold_in(key_of[7], 71), 0),
        "doc_blocks": jax.vmap(lambda own: uneven(own, DOCS, KEY_DEV // 128, KEY_DEV // 256, 2))(jax.random.split(key_of[6], N_ROW)).reshape((N_ROW, DOCS)).astype(jnp.int32),
    }


neg_large = -1e+30

def attend_block(queries_blk, pos_blk, pack_key_cache, pack_value_cache, doc_blocks):
    window_length = KEY_DEV
    heads_per_group = QUERY_HEADS // KEY_VALUE_HEADS
    key_index = jnp.arange(window_length, dtype=jnp.int32)
    score_scale = 1.0 / math.sqrt(HEAD_SIZE)

    def single(single_query_row, position):
        server = (position // window_length).astype(jnp.int32)
        offset = position - server * window_length
        first_row_index = (server * window_length).astype(jnp.int32)
        picked_key_rows = lax.dynamic_slice_in_dim(pack_key_cache, first_row_index, window_length, 0).reshape(window_length, KEY_VALUE_HEADS, HEAD_SIZE)
        picked_value_rows = lax.dynamic_slice_in_dim(pack_value_cache, first_row_index, window_length, 0).reshape(window_length, KEY_VALUE_HEADS, HEAD_SIZE)
        doc_ends = jnp.cumsum(doc_blocks[server]) * 128
        key_doc = lax.optimization_barrier(jnp.sum((key_index[:, None] >= doc_ends[None, :]).astype(jnp.int32), axis=1))
        query_doc = jnp.sum((offset >= doc_ends).astype(jnp.int32))
        allowed = (key_index <= offset) & (key_doc == query_doc)
        head_count = single_query_row.reshape(KEY_VALUE_HEADS, heads_per_group, HEAD_SIZE).astype(jnp.float32)
        scores = jnp.einsum('agd,kad->agk', head_count, picked_key_rows.astype(jnp.float32)) * score_scale
        scores = jnp.where(allowed[None, None, :], scores, neg_large)
        top_score = lax.optimization_barrier(jnp.max(scores, axis=2, keepdims=True))
        weights = jnp.where(allowed[None, None, :], jnp.exp(scores - top_score), 0.0)
        sums = lax.optimization_barrier(jnp.sum(weights, axis=2, keepdims=True))
        rounded = weights.astype(jnp.bfloat16).astype(jnp.float32)
        mixed_heads = jnp.einsum('agk,kad->agd', rounded, picked_value_rows.astype(jnp.float32))
        return (mixed_heads / sums).astype(jnp.bfloat16).reshape(QUERY_HEADS * HEAD_SIZE)
    return jax.vmap(single)(queries_blk, pos_blk)

def reference(hidden_rows, w_query, w_out, pack_key_cache, pack_value_cache, query_pos, doc_blocks):
    queries = jnp.dot(hidden_rows, w_query, preferred_element_type=jnp.float32).astype(jnp.bfloat16)
    block_rows = 4
    count = QROWS // block_rows

    def per_block(packed):
        return attend_block(packed[0], packed[1], pack_key_cache, pack_value_cache, doc_blocks)
    attended = lax.map(per_block, (queries.reshape(count, block_rows, QUERY_HEADS * HEAD_SIZE), query_pos.reshape(count, block_rows)))
    attended = attended.reshape(QROWS, QUERY_HEADS * HEAD_SIZE)
    part_width = QUERY_HEADS * HEAD_SIZE // N_TENSOR
    running = jnp.zeros((QROWS, D), jnp.float32)
    for group_idx in range(N_TENSOR):
        lower = group_idx * part_width
        term = jnp.dot(attended[:, lower:lower + part_width], w_out[lower:lower + part_width], preferred_element_type=jnp.float32).astype(jnp.bfloat16)
        term = lax.optimization_barrier(term)
        running = running + term.astype(jnp.float32)
    return running.astype(jnp.bfloat16)
```

```python
import math

import jax
import jax.numpy as jnp
from jax import lax
from jax.experimental import pallas as pl
from jax.experimental.pallas import tpu as pltpu
from jax.sharding import PartitionSpec as P

QUERY_HEADS = 64
KEY_VALUE_HEADS = 8
HEAD_SIZE = 128
HEADS_PER_GROUP = QUERY_HEADS // KEY_VALUE_HEADS
LANES = 128
SLOT_TILE = 32
KEY_TILE = 512
QUERY_CHUNKS = 2
OUT_CHUNKS = 4

neg_large = -1e30


def attend_kernel(lo_ref, hi_ref, q_ref, k_ref, v_ref, off_ref, start_ref, o_ref, s_ref):
    slots = q_ref.shape[0]
    kv_local = k_ref.shape[1] // HEAD_SIZE
    tile = SLOT_TILE
    rows = HEADS_PER_GROUP * tile
    span = s_ref.shape[3]
    factor = math.log2(math.e) / math.sqrt(HEAD_SIZE)

    def head_cols(a, g):
        return pl.ds((a * HEADS_PER_GROUP + g) * HEAD_SIZE, HEAD_SIZE)

    def one_tile(i, carry):
        here = pl.ds(pl.multiple_of(i * tile, tile), tile)
        lo, hi = lo_ref[i], hi_ref[i]
        off = off_ref[here, :]
        start = start_ref[here, :]
        queries = [
            jnp.concatenate([q_ref[here, head_cols(a, g)] for g in range(HEADS_PER_GROUP)], axis=0)
            for a in range(kv_local)
        ]

        def score(kb, tops):
            base = pl.multiple_of(kb * span, span)
            key_index = base + lax.broadcasted_iota(jnp.int32, (tile, span), 1)
            allowed = ((key_index >= start) & (key_index <= off))[None]
            new = []
            for a in range(kv_local):
                keys = k_ref[pl.ds(base, span), pl.ds(a * HEAD_SIZE, HEAD_SIZE)]
                s = lax.dot_general(
                    queries[a], keys, (((1,), (1,)), ((), ())), preferred_element_type=jnp.float32
                )
                s = jnp.where(allowed, s.reshape(HEADS_PER_GROUP, tile, span), neg_large)
                s = s.reshape(rows, span)
                s_ref[kb, a] = s
                top = tops[a]
                for c in range(span // LANES):
                    top = jnp.maximum(top, s[:, c * LANES : (c + 1) * LANES])
                new.append(top)
            return tuple(new)

        tops = lax.fori_loop(
            lo, hi, score, (jnp.full((rows, LANES), neg_large, jnp.float32),) * kv_local
        )
        tops = [jnp.max(top, axis=1, keepdims=True) for top in tops]

        def mix(kb, carry):
            base = pl.multiple_of(kb * span, span)
            new = []
            for a in range(kv_local):
                sums, total = carry[a]
                weights = jnp.exp2((s_ref[kb, a] - tops[a]) * factor)
                for c in range(span // LANES):
                    sums = sums + weights[:, c * LANES : (c + 1) * LANES]
                values = v_ref[pl.ds(base, span), pl.ds(a * HEAD_SIZE, HEAD_SIZE)]
                total = total + jnp.dot(
                    weights.astype(jnp.bfloat16), values, preferred_element_type=jnp.float32
                )
                new.append((sums, total))
            return tuple(new)

        zeros = (jnp.zeros((rows, LANES), jnp.float32), jnp.zeros((rows, HEAD_SIZE), jnp.float32))
        mixed = lax.fori_loop(lo, hi, mix, (zeros,) * kv_local)
        for a in range(kv_local):
            sums, total = mixed[a]
            sums = jnp.sum(sums, axis=1, keepdims=True)
            out = (total / jnp.where(sums > 0.0, sums, 1.0)).astype(jnp.bfloat16)
            for g in range(HEADS_PER_GROUP):
                o_ref[here, head_cols(a, g)] = out[g * tile : (g + 1) * tile]
        return carry

    lax.fori_loop(0, slots // tile, one_tile, 0)


def attend(queries, keys, values, offsets, starts, valid):
    slots, width = queries.shape
    key_span = keys.shape[0]
    kv_local = keys.shape[1] // HEAD_SIZE
    span = min(KEY_TILE, key_span)
    tiles = slots // SLOT_TILE
    by_tile = lambda x: x.reshape(tiles, SLOT_TILE)
    lo = jnp.min(by_tile(jnp.where(valid, starts, key_span)), axis=1)
    hi = jnp.max(by_tile(jnp.where(valid, offsets, -1)), axis=1)
    some = hi >= 0
    lo = jnp.where(some, lo // span, 0)
    hi = jnp.where(some, hi // span + 1, 0)
    vmem = pl.BlockSpec(memory_space=pltpu.VMEM)
    smem = pl.BlockSpec(memory_space=pltpu.SMEM)
    rows = HEADS_PER_GROUP * SLOT_TILE
    return pl.pallas_call(
        attend_kernel,
        out_shape=jax.ShapeDtypeStruct((slots, width), jnp.bfloat16),
        in_specs=[smem, smem, vmem, vmem, vmem, vmem, vmem],
        out_specs=vmem,
        scratch_shapes=[pltpu.VMEM((key_span // span, kv_local, rows, span), jnp.float32)],
        compiler_params=pltpu.CompilerParams(vmem_limit_bytes=52 * 2**20),
        cost_estimate=pl.CostEstimate(
            flops=slots * width * key_span,
            bytes_accessed=4 * slots * width + 4 * key_span * keys.shape[1],
            transcendentals=slots * width * key_span // HEAD_SIZE // 4,
        ),
        name="attend",
    )(lo, hi, queries, keys, values, offsets[:, None], starts[:, None])


def exact_pick(selection, table):
    return jnp.dot(
        selection.astype(jnp.bfloat16), table, preferred_element_type=jnp.float32
    ).astype(jnp.bfloat16)


def body(hidden_rows, w_query, w_out, pack_key_cache, pack_value_cache, query_pos, doc_blocks):
    servers = lax.axis_size("row")
    groups = lax.axis_size("tensor")
    row_count = hidden_rows.shape[0]
    key_span = pack_key_cache.shape[0]
    capacity = 2 * row_count // servers
    slot_count = servers * capacity
    head_width = w_query.shape[1]

    target = query_pos // key_span
    row_index = jnp.arange(row_count, dtype=jnp.int32)
    earlier = (target[:, None] == target[None, :]) & (row_index[None, :] < row_index[:, None])
    slot_index = target * capacity + jnp.sum(earlier.astype(jnp.int32), axis=1)
    slot_ids = jnp.arange(slot_count, dtype=jnp.int32)
    route = slot_ids[:, None] == slot_index[None, :]
    local = query_pos - target * key_span
    out_offset = jnp.sum(jnp.where(route, local[None, :] + 1, 0), axis=1) - 1
    offsets = lax.all_to_all(
        out_offset.reshape(servers, capacity), "row", split_axis=0, concat_axis=0, tiled=True
    ).reshape(slot_count)

    sort_key = jnp.where(offsets >= 0, offsets, key_span) * slot_count + slot_ids
    place = jnp.sum((sort_key[None, :] < sort_key[:, None]).astype(jnp.int32), axis=1)
    order = slot_ids[:, None] == place[None, :]
    sorted_offsets = jnp.sum(jnp.where(order, offsets[None, :] + 1, 0), axis=1) - 1
    doc_ends = jnp.cumsum(doc_blocks[0]) * 128
    starts = jnp.max(
        jnp.where(doc_ends[None, :] <= sorted_offsets[:, None], doc_ends[None, :], 0), axis=1
    )
    valid = sorted_offsets >= 0

    query_parts = []
    step = head_width // QUERY_CHUNKS
    gathered = None
    for c in range(QUERY_CHUNKS):
        part = w_query[:, c * step : (c + 1) * step]
        if gathered is not None:
            part, gathered = lax.optimization_barrier((part, gathered))
            query_parts.append(
                jnp.dot(hidden_rows, gathered, preferred_element_type=jnp.float32).astype(
                    jnp.bfloat16
                )
            )
        gathered = lax.all_gather(part, "row", axis=0, tiled=True)
    out_parts = []
    out_step = w_out.shape[1] // OUT_CHUNKS
    for c in range(OUT_CHUNKS):
        part = w_out[:, c * out_step : (c + 1) * out_step]
        if c == 0:
            part, gathered = lax.optimization_barrier((part, gathered))
            query_parts.append(
                jnp.dot(hidden_rows, gathered, preferred_element_type=jnp.float32).astype(
                    jnp.bfloat16
                )
            )
        else:
            part, out_parts[-1] = lax.optimization_barrier((part, out_parts[-1]))
        out_parts.append(lax.all_gather(part, "row", axis=1, tiled=True))

    queries = jnp.concatenate(query_parts, axis=1)
    outgoing = exact_pick(route, queries)
    incoming = lax.all_to_all(
        outgoing.reshape(servers, capacity, head_width),
        "row",
        split_axis=0,
        concat_axis=0,
        tiled=True,
    ).reshape(slot_count, head_width)
    sorted_queries = exact_pick(order, incoming)
    attended = attend(
        sorted_queries, pack_key_cache, pack_value_cache, sorted_offsets, starts, valid
    )
    attended = exact_pick(order.T, attended)
    returned = lax.all_to_all(
        attended.reshape(servers, capacity, head_width),
        "row",
        split_axis=0,
        concat_axis=0,
        tiled=True,
    ).reshape(slot_count, head_width)
    own_rows = exact_pick(route.T, returned)

    pieces = []
    shares = servers // groups
    for c in range(OUT_CHUNKS):
        partial = jnp.dot(
            own_rows, out_parts[c], preferred_element_type=jnp.float32
        ).astype(jnp.bfloat16)
        partial = jnp.stack(jnp.split(partial, groups, axis=1))
        shared = lax.all_to_all(partial, "tensor", split_axis=0, concat_axis=0, tiled=True)
        piece = jnp.sum(shared.astype(jnp.float32), axis=0).astype(jnp.bfloat16)
        pieces.append(piece.reshape(row_count, shares, out_step))
    return jnp.stack(pieces, axis=2).reshape(row_count, shares * w_out.shape[1])


def solution(mesh):
    return jax.shard_map(
        body,
        mesh=mesh,
        in_specs=(
            P("row", None),
            P("row", "tensor"),
            P("tensor", "row"),
            P("row", "tensor"),
            P("row", "tensor"),
            P("row"),
            P("row", None),
        ),
        out_specs=P("row", "tensor"),
        check_vma=False,
    )
```

```python
import math

import jax
import jax.numpy as jnp
from jax import lax
from jax.experimental import pallas as pl
from jax.experimental.pallas import tpu as pltpu
from jax.sharding import PartitionSpec as P

QUERY_HEADS = 64
KEY_VALUE_HEADS = 8
HEAD_SIZE = 128
HEADS_PER_GROUP = QUERY_HEADS // KEY_VALUE_HEADS
LANES = 128
SLOT_TILE = 32
KEY_TILE = 512
OUT_CUTS = (0, 2, 5, 8)

neg_large = -1e30


def attend_kernel(lo_ref, hi_ref, q_ref, k_ref, v_ref, off_ref, start_ref, o_ref, s_ref):
    slots = q_ref.shape[0]
    kv_local = k_ref.shape[1] // HEAD_SIZE
    tile = SLOT_TILE
    rows = HEADS_PER_GROUP * tile
    span = s_ref.shape[3]
    factor = math.log2(math.e) / math.sqrt(HEAD_SIZE)

    def head_cols(a, g):
        return pl.ds((a * HEADS_PER_GROUP + g) * HEAD_SIZE, HEAD_SIZE)

    def one_tile(i, carry):
        here = pl.ds(pl.multiple_of(i * tile, tile), tile)
        lo, hi = lo_ref[i], hi_ref[i]
        off = off_ref[here, :]
        start = start_ref[here, :]
        queries = [
            jnp.concatenate([q_ref[here, head_cols(a, g)] for g in range(HEADS_PER_GROUP)], axis=0)
            for a in range(kv_local)
        ]

        def score(kb, tops):
            base = pl.multiple_of(kb * span, span)
            key_index = base + lax.broadcasted_iota(jnp.int32, (tile, span), 1)
            allowed = ((key_index >= start) & (key_index <= off))[None]
            new = []
            for a in range(kv_local):
                keys = k_ref[pl.ds(base, span), pl.ds(a * HEAD_SIZE, HEAD_SIZE)]
                s = lax.dot_general(
                    queries[a], keys, (((1,), (1,)), ((), ())), preferred_element_type=jnp.float32
                )
                s = jnp.where(allowed, s.reshape(HEADS_PER_GROUP, tile, span), neg_large)
                s = s.reshape(rows, span)
                s_ref[kb, a] = s
                top = tops[a]
                for c in range(span // LANES):
                    top = jnp.maximum(top, s[:, c * LANES : (c + 1) * LANES])
                new.append(top)
            return tuple(new)

        tops = lax.fori_loop(
            lo, hi, score, (jnp.full((rows, LANES), neg_large, jnp.float32),) * kv_local
        )
        tops = [jnp.max(top, axis=1, keepdims=True) for top in tops]

        def mix(kb, carry):
            base = pl.multiple_of(kb * span, span)
            new = []
            for a in range(kv_local):
                sums, total = carry[a]
                weights = jnp.exp2((s_ref[kb, a] - tops[a]) * factor)
                for c in range(span // LANES):
                    sums = sums + weights[:, c * LANES : (c + 1) * LANES]
                values = v_ref[pl.ds(base, span), pl.ds(a * HEAD_SIZE, HEAD_SIZE)]
                total = total + jnp.dot(
                    weights.astype(jnp.bfloat16), values, preferred_element_type=jnp.float32
                )
                new.append((sums, total))
            return tuple(new)

        zeros = (jnp.zeros((rows, LANES), jnp.float32), jnp.zeros((rows, HEAD_SIZE), jnp.float32))
        mixed = lax.fori_loop(lo, hi, mix, (zeros,) * kv_local)
        for a in range(kv_local):
            sums, total = mixed[a]
            sums = jnp.sum(sums, axis=1, keepdims=True)
            out = (total / jnp.where(sums > 0.0, sums, 1.0)).astype(jnp.bfloat16)
            for g in range(HEADS_PER_GROUP):
                o_ref[here, head_cols(a, g)] = out[g * tile : (g + 1) * tile]
        return carry

    lax.fori_loop(0, slots // tile, one_tile, 0)


def attend(queries, keys, values, offsets, starts, valid):
    slots, width = queries.shape
    key_span = keys.shape[0]
    kv_local = keys.shape[1] // HEAD_SIZE
    span = min(KEY_TILE, key_span)
    tiles = slots // SLOT_TILE
    by_tile = lambda x: x.reshape(tiles, SLOT_TILE)
    lo = jnp.min(by_tile(jnp.where(valid, starts, key_span)), axis=1)
    hi = jnp.max(by_tile(jnp.where(valid, offsets, -1)), axis=1)
    some = hi >= 0
    lo = jnp.where(some, lo // span, 0)
    hi = jnp.where(some, hi // span + 1, 0)
    vmem = pl.BlockSpec(memory_space=pltpu.VMEM)
    smem = pl.BlockSpec(memory_space=pltpu.SMEM)
    rows = HEADS_PER_GROUP * SLOT_TILE
    return pl.pallas_call(
        attend_kernel,
        out_shape=jax.ShapeDtypeStruct((slots, width), jnp.bfloat16),
        in_specs=[smem, smem, vmem, vmem, vmem, vmem, vmem],
        out_specs=vmem,
        scratch_shapes=[pltpu.VMEM((key_span // span, kv_local, rows, span), jnp.float32)],
        compiler_params=pltpu.CompilerParams(vmem_limit_bytes=52 * 2**20),
        cost_estimate=pl.CostEstimate(
            flops=slots * width * key_span,
            bytes_accessed=4 * slots * width + 4 * key_span * keys.shape[1],
            transcendentals=slots * width * key_span // HEAD_SIZE // 4,
        ),
        name="attend",
    )(lo, hi, queries, keys, values, offsets[:, None], starts[:, None])


def exact_pick(selection, table):
    return jnp.dot(
        selection.astype(jnp.bfloat16), table, preferred_element_type=jnp.float32
    ).astype(jnp.bfloat16)


def body(hidden_rows, w_query, w_out, pack_key_cache, pack_value_cache, query_pos, doc_blocks):
    servers = lax.axis_size("row")
    groups = lax.axis_size("tensor")
    row_count = hidden_rows.shape[0]
    key_span = pack_key_cache.shape[0]
    capacity = 2 * row_count // servers
    slot_count = servers * capacity
    head_width = w_query.shape[1]

    target = query_pos // key_span
    row_index = jnp.arange(row_count, dtype=jnp.int32)
    earlier = (target[:, None] == target[None, :]) & (row_index[None, :] < row_index[:, None])
    slot_index = target * capacity + jnp.sum(earlier.astype(jnp.int32), axis=1)
    slot_ids = jnp.arange(slot_count, dtype=jnp.int32)
    route = slot_ids[:, None] == slot_index[None, :]
    local = query_pos - target * key_span
    out_offset = jnp.sum(jnp.where(route, local[None, :] + 1, 0), axis=1) - 1
    offsets = lax.all_to_all(
        out_offset.reshape(servers, capacity), "row", split_axis=0, concat_axis=0, tiled=True
    ).reshape(slot_count)

    sort_key = jnp.where(offsets >= 0, offsets, key_span) * slot_count + slot_ids
    place = jnp.sum((sort_key[None, :] < sort_key[:, None]).astype(jnp.int32), axis=1)
    order = slot_ids[:, None] == place[None, :]
    sorted_offsets = jnp.sum(jnp.where(order, offsets[None, :] + 1, 0), axis=1) - 1
    doc_ends = jnp.cumsum(doc_blocks[0]) * 128
    starts = jnp.max(
        jnp.where(doc_ends[None, :] <= sorted_offsets[:, None], doc_ends[None, :], 0), axis=1
    )
    valid = sorted_offsets >= 0

    columns = jnp.stack(jnp.split(hidden_rows, servers, axis=1))
    columns = lax.all_to_all(columns, "row", split_axis=0, concat_axis=0, tiled=True)
    columns = columns.reshape(servers * row_count, w_query.shape[0])
    bounds = [w_out.shape[1] * cut // 8 for cut in OUT_CUTS]
    first, *later = [w_out[:, lower:upper] for lower, upper in zip(bounds, bounds[1:])]
    first = lax.all_gather(first, "row", axis=1, tiled=True)
    columns, first, route, order, sorted_offsets, starts, valid = lax.optimization_barrier(
        (columns, first, route, order, sorted_offsets, starts, valid)
    )
    shares_sum = lax.psum_scatter(
        jnp.dot(columns, w_query, preferred_element_type=jnp.float32),
        "row",
        scatter_dimension=0,
        tiled=True,
    )
    later, shares_sum = lax.optimization_barrier((tuple(later), shares_sum))
    out_parts = [first] + [lax.all_gather(part, "row", axis=1, tiled=True) for part in later]
    queries = shares_sum.astype(jnp.bfloat16)
    outgoing = exact_pick(route, queries)
    incoming = lax.all_to_all(
        outgoing.reshape(servers, capacity, head_width),
        "row",
        split_axis=0,
        concat_axis=0,
        tiled=True,
    ).reshape(slot_count, head_width)
    sorted_queries = exact_pick(order, incoming)
    attended = attend(
        sorted_queries, pack_key_cache, pack_value_cache, sorted_offsets, starts, valid
    )
    attended = exact_pick(order.T, attended)
    returned = lax.all_to_all(
        attended.reshape(servers, capacity, head_width),
        "row",
        split_axis=0,
        concat_axis=0,
        tiled=True,
    ).reshape(slot_count, head_width)
    own_rows = exact_pick(route.T, returned)

    pieces = []
    shares = servers // groups
    for part in out_parts:
        partial = jnp.dot(
            own_rows, part, preferred_element_type=jnp.float32
        ).astype(jnp.bfloat16)
        if part is out_parts[-1]:
            piece = lax.psum_scatter(partial, "tensor", scatter_dimension=1, tiled=True)
        else:
            partial = jnp.stack(jnp.split(partial, groups, axis=1))
            shared = lax.all_to_all(partial, "tensor", split_axis=0, concat_axis=0, tiled=True)
            piece = jnp.sum(shared.astype(jnp.float32), axis=0).astype(jnp.bfloat16)
        pieces.append(piece.reshape(row_count, shares, part.shape[1] // servers))
    return jnp.concatenate(pieces, axis=2).reshape(row_count, shares * w_out.shape[1])


def solution(mesh):
    return jax.shard_map(
        body,
        mesh=mesh,
        in_specs=(
            P("row", None),
            P("row", "tensor"),
            P("tensor", "row"),
            P("row", "tensor"),
            P("row", "tensor"),
            P("row"),
            P("row", None),
        ),
        out_specs=P("row", "tensor"),
        check_vma=False,
    )
```
